128 devices in a mesh: dp: 16 (over x, y_lo, core), seq: 8 (over z, y_hi).
Axes of the slice: x: 4, y: 4 (y_hi: 2, y_lo: 2; y = y_hi * 2 + y_lo), z: 4, core: 2. Of those that a mesh axis runs over, the one named last changes fastest.
Arguments:
- queries: bfloat16 [16, 2048, 2048], P('dp', 'seq'), may hold values from -6 to 6
- keys: bfloat16 [16, 2048, 1024], P('dp', 'seq'), may hold values from -6 to 6
- values: bfloat16 [16, 2048, 1024], P('dp', 'seq'), may hold values from -190 to 190
- segments: int32 [16, 2048], P('dp', 'seq'), may hold values from 0 to 2, never falling along the last dimension, each value on 1 to 1280 neighbouring positions
- cotangent: bfloat16 [16, 2048, 2304], P('dp', 'seq'), may hold values from -6 to 6
- weight: float32 [2048, 2304], P(('dp', 'seq')), may hold values from -0.125 to 0.125
- first_moment: bfloat16 [2048, 2304], P(('dp', 'seq')), may hold values from -1 to 1
- first_scale: float32 [2048, 18], P(('dp', 'seq')), may hold values from 0.3 to 3
- second_moment: bfloat16 [2048, 2304], P(('dp', 'seq')), may hold values from 0.049804688 to 1
- second_scale: float32 [2048, 18], P(('dp', 'seq')), may hold values from 0.3 to 3
Outputs:
- layer_out: bfloat16 [16, 2048, 2304], P('dp', 'seq')
- new_weight: float32 [2048, 2304], P(('dp', 'seq'))
- new_first: bfloat16 [2048, 2304], P(('dp', 'seq'))
- new_first_scale: float32 [2048, 18], P(('dp', 'seq'))
- new_second: bfloat16 [2048, 2304], P(('dp', 'seq'))
- new_second_scale: float32 [2048, 18], P(('dp', 'seq'))
The draws below stay inside these ranges and needn't reach their ends.
Inputs may be any that keep to these rules, and one draw needn't show every extreme that they name: `segments`: document numbers never fall along a sequence; each sequence holds 3 documents, one of exactly 1280 positions.
All inputs are finite; a program needn't handle non-finite values. Where the reference program divides by a largest or mean magnitude, that divisor is 1e-20 or more.
Results may differ from the reference program's by a relative error of at most 0.01.
Values may be sent and summed in bfloat16 or wider, within the bound.
No kernel may reach another device: no remote copies, remote signals or barrier semaphores. Data moves between devices by JAX's collectives and lax.ppermute only.
A program may use at most 128 MiB of HBM per device.

```python
import math
import jax
import jax.numpy as jnp
import numpy as np
from jax import lax

HEADS = 16
KV_HEADS = 8
HEAD_DIM = 128
DO = 2304
GROUP = 128
DOCS = 3
QW = 2048
KW = 1024
LENGTH = 2048
SEQS = 16
DOC_MOST = 1280


def draw_values(key, part):
    base_key, column_key, row_key = jax.random.split(jax.random.fold_in(key, 17), 3)
    columns = jnp.arange(KW, dtype=jnp.float32)
    column_multiplier = 10.0 ** (columns / (KW - 1)) * jax.random.uniform(column_key, (KW,), jnp.float32, 0.7, 1.4)
    row_factor = jnp.exp(jax.random.uniform(row_key, (SEQS, LENGTH, 1), jnp.float32, 0.0, math.log(10.0)))
    base = jnp.clip(jax.random.normal(base_key, (SEQS, LENGTH, KW), jnp.float32), -4.0, 4.0)
    return (base * column_multiplier * row_factor / 3.0).astype(jnp.bfloat16)


def level_of(stream_key, dims, shards, smallest, largest):
    def one(dim, shards_of):
        heights = jax.random.uniform(jax.random.fold_in(jax.random.fold_in(stream_key, 6), dim), (shards_of,), jnp.float32, smallest / len(shards), largest / len(shards))
        return jnp.repeat(jnp.exp(heights), dims[dim] // shards_of).reshape((-1,) + (1,) * (len(dims) - dim - 1))

    loudness = one(*shards[0])
    for cut in shards[1:]:
        loudness = loudness * one(*cut)
    return loudness


def length_profile(number_of, total, reach, slope):
    loads = [(1 << 20) // math.isqrt(rank ** slope) + 1 for rank in range(2, number_of + 1)]
    spare, holding = total - reach - (number_of - 1), [1] * (number_of - 1)
    while spare > 0:
        candidates = [i for i in range(number_of - 1) if holding[i] < reach]
        mass, budget = sum([loads[i] for i in candidates]), spare
        for i in candidates:
            addition = min(reach - holding[i], max(1, budget * loads[i] // mass), spare)
            holding[i] = holding[i] + addition
            spare = spare - addition
    return np.array([reach] + holding)


def uneven(own_key, number_of, total, most, lean):
    if number_of == 2:
        one = jax.random.randint(own_key, (), max(1, total - most), min(most, total - 1) + 1)
        return jnp.stack([one, total - one])
    sizes = jnp.asarray(length_profile(number_of, total, most, lean), jnp.int32)
    twos = (number_of - 1) // 2
    giver, sink = sizes[1:1 + 2 * twos:2], sizes[2:2 + 2 * twos:2]
    margin = jnp.minimum(giver - 1, most - sink)
    passed = jax.random.randint(jax.random.fold_in(own_key, 1), (twos,), 0, 1 << 20) % (margin + 1)
    sizes = sizes.at[1:1 + 2 * twos:2].set(giver - passed).at[2:2 + 2 * twos:2].set(sink + passed)
    return sizes[jax.random.permutation(jax.random.fold_in(own_key, 2), number_of)]


def bell_draw(stream_key, dims, width, limit, pieces=(), held_as=jnp.bfloat16):
    drawn = width * jax.random.normal(stream_key, dims, jnp.float32)
    if pieces:
        drawn = drawn * level_of(stream_key, dims, pieces, -0.22, 0.18)
    return jnp.clip(drawn, -limit, limit).astype(held_as)


def setup_inputs(seed: int = 0) -> dict:
    seeds = jax.random.split(jax.random.key(seed), 11)
    queries = bell_draw(seeds[0], (SEQS, LENGTH, QW), 1.0, 6.0, ((0, 16), (1, 8)))
    keys = bell_draw(seeds[1], (SEQS, LENGTH, KW), 1.0, 6.0, ((0, 16), (1, 8)))
    values = draw_values(jax.random.fold_in(seeds[10], 71), 0)
    segments = jax.vmap(lambda own: jnp.searchsorted(jnp.cumsum(uneven(own, DOCS, LENGTH, DOC_MOST, 0)), jnp.arange(LENGTH), side="right"))(jax.random.split(seeds[3], SEQS)).reshape((SEQS, LENGTH)).astype(jnp.int32)
    cotangent = bell_draw(seeds[4], (SEQS, LENGTH, DO), 1.0, 6.0, ((0, 16), (1, 8)))
    weight = bell_draw(seeds[5], (QW, DO), QW ** -0.5, 0.125, ((0, 128),), jnp.float32)
    first_moment = jnp.clip(jax.random.uniform(seeds[6], (QW, DO), jnp.float32, -1.0, 1.0) * level_of(seeds[6], (QW, DO), ((0, 128),), -0.4, 0.0), -1.0, 1.0).astype(jnp.bfloat16)
    first_scale = jnp.clip(jnp.exp(math.log(3.0) - 2.3025851 * jax.random.uniform(seeds[7], (QW, DO // GROUP), jnp.float32) ** level_of(seeds[7], (QW, DO // GROUP), ((0, 128),), -0.2, 0.2)), 0.3, 3.0)
    second_moment = jnp.clip(0.049804688 + 0.9501953 * jax.random.uniform(seeds[8], (QW, DO), jnp.float32) ** level_of(seeds[8], (QW, DO), ((0, 128),), -0.2, 0.2), 0.049804688, 1.0).astype(jnp.bfloat16)
    second_scale = jnp.clip(jnp.exp(math.log(3.0) - 2.3025851 * jax.random.uniform(seeds[9], (QW, DO // GROUP), jnp.float32) ** level_of(seeds[9], (QW, DO // GROUP), ((0, 128),), -0.2, 0.2)), 0.3, 3.0)
    return dict(queries=queries, keys=keys, values=values, segments=segments, cotangent=cotangent, weight=weight, first_moment=first_moment, first_scale=first_scale, second_moment=second_moment, second_scale=second_scale)


score_scale = 144.0 ** (-0.5)
soft_cap = 50.0
beta_first = 0.9
beta_second = 0.95
learn_rate = 0.001
decay_rate = 0.1

def quantize(blocks):
    grouped = blocks.astype(jnp.float32).reshape(blocks.shape[0], KV_HEADS, HEAD_DIM)
    scales = (lax.optimization_barrier(jnp.max(jnp.abs(grouped), axis=-1)) + 1e-06).astype(jnp.bfloat16)
    coded = (grouped / scales.astype(jnp.float32)[..., None]).astype(jnp.bfloat16)
    return (coded, scales)

def recover_values(coded, scales):
    return (coded.astype(jnp.float32) * scales.astype(jnp.float32)[..., None]).astype(jnp.bfloat16)

def attend(packed):
    query_seq, key_seq, value_seq, docs_seq = packed
    length = query_seq.shape[0]
    key_code, key_scale = quantize(key_seq)
    value_code, value_scale = quantize(value_seq)
    key_estimate = lax.optimization_barrier(recover_values(key_code, key_scale)).astype(jnp.float32)
    value_hat = lax.optimization_barrier(recover_values(value_code, value_scale)).astype(jnp.float32)
    grouped = query_seq.astype(jnp.float32).reshape(length, KV_HEADS, HEADS // KV_HEADS, HEAD_DIM)
    scores = jnp.einsum('qgrd,kgd->qgrk', grouped, key_estimate) * score_scale
    capped = soft_cap * jnp.tanh(scores / soft_cap)
    places = jnp.arange(length, dtype=jnp.int32)
    allowed = (docs_seq[:, None] == docs_seq[None, :]) & (places[None, :] <= places[:, None])
    weights = jnp.where(allowed[:, None, None, :], jnp.exp(capped), jnp.float32(0.0))
    totals = lax.optimization_barrier(jnp.sum(weights, axis=-1))
    rounded = lax.optimization_barrier(weights.astype(jnp.bfloat16)).astype(jnp.float32)
    mixed = jnp.einsum('qgrk,kgd->qgrd', rounded, value_hat)
    return (mixed / totals[..., None]).reshape(length, HEADS * HEAD_DIM).astype(jnp.bfloat16)

def decode(coded, scales):
    values_f = coded.astype(jnp.float32).reshape(coded.shape[0], -1, GROUP)
    return (scales[..., None] * jnp.sign(values_f) * jnp.sqrt(jnp.abs(values_f))).reshape(coded.shape)

def encode(moment):
    grouped = moment.reshape(moment.shape[0], -1, GROUP)
    scales = lax.optimization_barrier(jnp.max(jnp.abs(grouped), axis=-1)) + 1e-06
    coded = (grouped * jnp.abs(grouped) / (scales[..., None] * scales[..., None])).astype(jnp.bfloat16)
    return (coded.reshape(moment.shape), scales)

def reference(queries, keys, values, segments, cotangent, weight, first_moment, first_scale, second_moment, second_scale):
    attended = lax.map(attend, (queries, keys, values, segments))
    attended_flat = attended.reshape(-1, QW)
    weight_low = weight.astype(jnp.bfloat16)
    layer_out = jnp.dot(attended_flat, weight_low, preferred_element_type=jnp.float32).astype(jnp.bfloat16)
    layer_out = layer_out.reshape(SEQS, LENGTH, DO)
    gradient_matrix = jnp.dot(attended_flat.T, cotangent.reshape(-1, DO), preferred_element_type=jnp.float32)
    sum_squares = jnp.sum(gradient_matrix * gradient_matrix)
    rms_value = jnp.sqrt(sum_squares / (QW * DO) + 1e-06)
    clipped = gradient_matrix * jnp.minimum(jnp.float32(1.0), 1.0 / rms_value)
    first = beta_first * decode(first_moment, first_scale) + (1.0 - beta_first) * clipped
    second = beta_second * decode(second_moment, second_scale) + (1.0 - beta_second) * clipped * clipped
    new_weight = weight - learn_rate * (first / (jnp.sqrt(second) + 1e-08) + decay_rate * weight)
    new_first, new_first_scale = encode(first)
    new_second, new_second_scale = encode(second)
    return (layer_out, new_weight, new_first, new_first_scale, new_second, new_second_scale)
```

```python
import jax
import jax.numpy as jnp
from jax import lax
from jax.experimental import pallas as pl
from jax.experimental.pallas import tpu as pltpu
from jax.sharding import Mesh
from jax.sharding import PartitionSpec as P

QW = 2048
DO = 2304
GROUP = 128
TILE = 256
BLOCKS = 8
NOTE = 16
SEQ = ("seq_0", "seq_1")
DP = ("dp_0", "dp_1", "dp_2")
DP_SEQ = ("dp_0", "dp_1", "dp_2", "seq_0", "seq_1")
LOG2E = 1.4426950408889634
VMEM_LIMIT = 48 * 1024 * 1024

score_scale = 144.0 ** (-0.5)
soft_cap = 50.0
beta_first = 0.9
beta_second = 0.95
learn_rate = 0.001
decay_rate = 0.1

F32 = jnp.float32
BF16 = jnp.bfloat16


def params(*semantics):
    return pltpu.CompilerParams(
        vmem_limit_bytes=VMEM_LIMIT,
        dimension_semantics=semantics or None,
    )


def restored(entries):
    wide = entries.astype(F32)
    scale = (jnp.max(jnp.abs(wide), axis=-1, keepdims=True) + 1e-06).astype(BF16).astype(F32)
    coded = (wide / scale).astype(BF16).astype(F32)
    return (coded * scale).astype(BF16)


def pack_kernel(q_ref, k_ref, v_ref, seg_ref, out_ref):
    out_ref[0, :TILE, 0:256] = q_ref[...]
    out_ref[0, :TILE, 256:384] = restored(k_ref[...])
    out_ref[0, :TILE, 384:512] = restored(v_ref[...])
    seg = seg_ref[...]
    below_1 = jnp.sum((seg < 1).astype(F32), axis=-1, keepdims=True)
    below_2 = jnp.sum((seg < 2).astype(F32), axis=-1, keepdims=True)
    out_ref[0, TILE:, 0:256] = jnp.broadcast_to(below_1, (NOTE, 256)).astype(BF16)
    out_ref[0, TILE:, 256:512] = jnp.broadcast_to(below_2, (NOTE, 256)).astype(BF16)


def pack(q, k, v, seg):
    return pl.pallas_call(
        pack_kernel,
        grid=(BLOCKS,),
        in_specs=[
            pl.BlockSpec((TILE, 256), lambda h: (0, h)),
            pl.BlockSpec((TILE, 128), lambda h: (0, h)),
            pl.BlockSpec((TILE, 128), lambda h: (0, h)),
            pl.BlockSpec((1, TILE), lambda h: (0, 0)),
        ],
        out_specs=pl.BlockSpec((1, TILE + NOTE, 512), lambda h: (h, 0, 0)),
        out_shape=jax.ShapeDtypeStruct((BLOCKS, TILE + NOTE, 512), BF16),
        compiler_params=params("arbitrary"),
        name="pack",
    )(q, k, v, seg)


def attend_kernel(in_ref, out_ref, acc, total):
    notes = in_ref[:, TILE : TILE + 8, :].astype(F32).sum(axis=0)
    first_of_1 = jnp.max(notes[:, 0:128]).astype(jnp.int32)
    first_of_2 = jnp.max(notes[:, 256:384]).astype(jnp.int32)

    def first_seen(place):
        return jnp.where(
            place < first_of_1, 0, jnp.where(place < first_of_2, first_of_1, first_of_2)
        )

    key_row = lax.broadcasted_iota(jnp.int32, (TILE, 2 * TILE), 0)
    lane = lax.broadcasted_iota(jnp.int32, (1, 2 * TILE), 1)
    query_col = jnp.where(lane < TILE, lane, lane - TILE)

    for i in range(BLOCKS):
        query = jnp.concatenate([in_ref[i, :TILE, 0:128], in_ref[i, :TILE, 128:256]], axis=0)
        start_row = first_seen(i * TILE + query_col)
        start_low = first_seen(jnp.int32(i * TILE))
        start_high = first_seen(jnp.int32(i * TILE + TILE - 1))
        acc[...] = jnp.zeros_like(acc)
        total[...] = jnp.zeros_like(total)

        def step(j, mask, query=query):
            key = in_ref[j, :TILE, 256:384]
            value = in_ref[j, :TILE, 384:512]
            scores = lax.dot_general(
                key, query, (((1,), (1,)), ((), ())), preferred_element_type=F32
            )
            capped = jnp.tanh(scores * (score_scale / soft_cap))
            weights = jnp.exp2(capped * (soft_cap * LOG2E))
            if mask is not None:
                weights = jnp.where(mask, weights, 0.0)
            total[...] += weights.reshape(TILE // 8, 8, 2 * TILE).sum(axis=0)
            acc[...] += lax.dot_general(
                value, weights.astype(BF16), (((0,), (0,)), ((), ())), preferred_element_type=F32
            )

        low = start_low // TILE
        clear = jnp.minimum((start_high + TILE - 1) // TILE, i)

        @pl.loop(low, clear)
        def _(j):
            step(j, key_row + j * TILE >= start_row)

        @pl.loop(clear, i)
        def _(j):
            step(j, None)

        step(i, (key_row <= query_col) & (key_row + i * TILE >= start_row))

        attended = (acc[...] / jnp.sum(total[...], axis=0, keepdims=True)).astype(BF16)
        for x in range(4):
            for c in range(2):
                out_ref[(x * 2 + c) * BLOCKS + i] = attended[
                    x * 32 : (x + 1) * 32, c * TILE : (c + 1) * TILE
                ]


def attend(packed):
    return pl.pallas_call(
        attend_kernel,
        out_shape=jax.ShapeDtypeStruct((64, 32, TILE), BF16),
        in_specs=[pl.BlockSpec(memory_space=pltpu.VMEM)],
        out_specs=pl.BlockSpec(memory_space=pltpu.VMEM),
        scratch_shapes=[pltpu.VMEM((128, 2 * TILE), F32), pltpu.VMEM((8, 2 * TILE), F32)],
        compiler_params=params(),
        name="attend",
    )(packed)


def gradient_kernel(me_ref, att_ref, *refs):
    cots, out_ref = refs[:8], refs[8]
    x, c = me_ref[0], me_ref[2]
    total = jnp.zeros((256, TILE), F32)
    for core in range(2):
        for k in range(4):
            member = lax.rem(x - k + 4, 4) * 2 + (c if core == 0 else 1 - c)
            total += jnp.dot(
                att_ref[member], cots[core * 4 + k][...], preferred_element_type=F32
            )
    low = total.astype(BF16)
    for fx in range(4):
        for fy in range(2):
            for fh in range(2):
                row = ((fx * 2 + fy) * 2 + fh) * 16
                out_ref[(fy * 4 + fx) * 2 + fh] = low[row : row + 16]


def gradient_rows(me, att, cots):
    return pl.pallas_call(
        gradient_kernel,
        grid_spec=pltpu.PrefetchScalarGridSpec(
            num_scalar_prefetch=1,
            grid=(DO // TILE,),
            in_specs=[pl.BlockSpec((8, 256, TILE), lambda n, me: (0, 0, 0))]
            + [pl.BlockSpec((TILE, TILE), lambda n, me: (0, n))] * 8,
            out_specs=pl.BlockSpec((16, 16, TILE), lambda n, me: (0, 0, n)),
        ),
        out_shape=jax.ShapeDtypeStruct((16, 16, DO), BF16),
        compiler_params=params("arbitrary"),
        name="gradient_rows",
    )(me, att, *cots)


def project_kernel(me_ref, att_ref, *refs):
    rows, out_ref, left = refs[:8], refs[8], refs[9]
    x, c, z = me_ref[0], me_ref[2], me_ref[3]
    y = me_ref[4] * 2 + me_ref[1]

    @pl.when(pl.program_id(0) == 0)
    def _():
        for core in range(2):
            fc = c if core == 0 else 1 - c
            for kx in range(4):
                fx = lax.rem(x - kx + 4, 4)
                blocks = []
                for kz in range(4):
                    fz = lax.rem(z - kz + 4, 4)
                    for ky in range(4):
                        fy = lax.rem(y - ky + 4, 4)
                        low, high = lax.rem(fy, 2), fy // 2
                        blocks.append(att_ref[fz * 2 + fc, fx * 4 + low * 2 + high])
                left[core * 4 + kx] = jnp.concatenate(blocks, axis=0).T

    total = jnp.zeros((TILE, TILE), F32)
    for k in range(8):
        total += jnp.dot(left[k], rows[k][...], preferred_element_type=F32)
    out_ref[0] = total.astype(BF16)


def project(me, att, rows):
    return pl.pallas_call(
        project_kernel,
        grid_spec=pltpu.PrefetchScalarGridSpec(
            num_scalar_prefetch=1,
            grid=(DO // TILE,),
            in_specs=[pl.BlockSpec((8, 16, 16, TILE), lambda n, me: (0, 0, 0, 0))]
            + [pl.BlockSpec((TILE, TILE), lambda n, me: (0, n))] * 8,
            out_specs=pl.BlockSpec((1, TILE, TILE), lambda n, me: (0, 0, n)),
            scratch_shapes=[pltpu.VMEM((8, TILE, TILE), BF16)],
        ),
        out_shape=jax.ShapeDtypeStruct((1, TILE, DO), BF16),
        compiler_params=params("arbitrary"),
        name="project",
    )(me, att, *rows)


def total_kernel(parts_ref, grad_ref, squares_ref):
    total = parts_ref[0].astype(F32)
    for k in range(1, 16):
        total += parts_ref[k].astype(F32)
    grad_ref[...] = total
    squares = jnp.sum(total * total)
    squares_ref[...] = jnp.broadcast_to(squares, squares_ref.shape)


def total_rows(parts):
    return pl.pallas_call(
        total_kernel,
        out_shape=(
            jax.ShapeDtypeStruct((16, DO), F32),
            jax.ShapeDtypeStruct((128, 1, 128), F32),
        ),
        compiler_params=params(),
        name="total_rows",
    )(parts)


def adam_kernel(
    grad_ref, squares_ref, weight_ref, first_ref, fscale_ref, second_ref, sscale_ref,
    new_weight_ref, new_first_ref, new_fscale_ref, new_second_ref, new_sscale_ref,
):
    sum_squares = jnp.sum(squares_ref[:, 0, :]) * (1.0 / 128.0)
    rms = jnp.sqrt(jnp.full((16, GROUP), sum_squares * (1.0 / (QW * DO)) + 1e-06, F32))
    shrink = jnp.minimum(1.0, 1.0 / rms)

    def decode(coded, scale):
        magnitude = scale * jnp.sqrt(jnp.abs(coded))
        return jnp.where(coded < 0.0, -magnitude, magnitude)

    def encode(x):
        scale = jnp.max(jnp.abs(x), axis=-1, keepdims=True) + 1e-06
        return (x * jnp.abs(x) / (scale * scale)).astype(BF16), scale

    fscales, sscales = [], []
    for g in range(DO // GROUP):
        at = slice(g * GROUP, (g + 1) * GROUP)
        clipped = grad_ref[:, at] * shrink
        first_old = decode(first_ref[:, at].astype(F32), fscale_ref[:, g : g + 1])
        second_old = decode(second_ref[:, at].astype(F32), sscale_ref[:, g : g + 1])
        first = beta_first * first_old + (1.0 - beta_first) * clipped
        second = beta_second * second_old + (1.0 - beta_second) * clipped * clipped
        weight = weight_ref[:, at]
        new_weight_ref[:, at] = weight - learn_rate * (
            first / (jnp.sqrt(second) + 1e-08) + decay_rate * weight
        )
        new_first_ref[:, at], scale = encode(first)
        fscales.append(scale)
        new_second_ref[:, at], scale = encode(second)
        sscales.append(scale)
    new_fscale_ref[...] = jnp.concatenate(fscales, axis=1)
    new_sscale_ref[...] = jnp.concatenate(sscales, axis=1)


def adam(grad, squares, weight, first, fscale, second, sscale):
    return pl.pallas_call(
        adam_kernel,
        out_shape=tuple(
            jax.ShapeDtypeStruct(a.shape, a.dtype) for a in (weight, first, fscale, second, sscale)
        ),
        compiler_params=params(),
        name="adam",
    )(grad, squares, weight, first, fscale, second, sscale)


def shift(x, axis, by):
    peers = lax.axis_size(axis)
    return lax.ppermute(x, axis, [(i, (i + by) % peers) for i in range(peers)])


def shift_y(x, by):
    pairs = []
    for y in range(4):
        to = (y + by) % 4
        pairs.append(((y % 2) * 2 + y // 2, (to % 2) * 2 + to // 2))
    return lax.ppermute(x, ("dp_1", "seq_1"), pairs)


def from_along(x, move):
    return [x] + [move(x, k) for k in (1, 2, 3)]


def local(
    queries, keys, values, segments, cotangent, weight,
    first_moment, first_scale, second_moment, second_scale,
):
    me = jnp.stack([lax.axis_index(a) for a in DP_SEQ]).astype(jnp.int32)
    across = lambda v, k: shift(v, "dp_0", k)

    packed = pack(queries[0], keys[0], values[0], segments)
    arrived = lax.all_to_all(packed, SEQ, 0, 0, tiled=True)

    cots = from_along(cotangent[0], across)
    cots = cots + [shift(v, "dp_2", 1) for v in cots]

    rows = weight.astype(BF16)
    rows = jnp.concatenate(from_along(rows, shift_y), axis=0)
    rows = jnp.concatenate(from_along(rows, lambda v, k: shift(v, "seq_0", k)), axis=0)
    rows = from_along(rows, across)
    rows = rows + [shift(v, "dp_2", 1) for v in rows]

    attended = attend(arrived)
    columns = lax.all_to_all(
        attended, ("dp_0", "dp_2", "seq_0", "seq_1"), 0, 0, tiled=True
    ).reshape(8, 256, TILE)
    partial = gradient_rows(me, columns, cots)
    parts = lax.all_to_all(partial, ("dp_1", "seq_0", "seq_1"), 0, 0, tiled=True)
    grad, squares = total_rows(parts)
    swap = [
        ((x * 4 + z) , (z * 4 + x)) for x in range(4) for z in range(4)
    ]
    grad = lax.ppermute(grad, ("dp_0", "seq_0"), swap)
    squares = lax.all_to_all(squares, DP_SEQ, 0, 0, tiled=True)
    new_weight, new_first, new_fscale, new_second, new_sscale = adam(
        grad, squares, weight, first_moment, first_scale, second_moment, second_scale
    )
    own = lax.all_to_all(columns, ("dp_0", "dp_2"), 0, 0, tiled=True).reshape(8, 16, 16, TILE)
    layer_out = project(me, own, rows)
    return (layer_out, new_weight, new_first, new_fscale, new_second, new_sscale)


def solution(mesh):
    finer = Mesh(mesh.devices.reshape(4, 2, 2, 4, 2), DP_SEQ)
    tokens = P(DP, SEQ, None)
    rows = P(DP_SEQ, None)
    return jax.shard_map(
        local,
        mesh=finer,
        in_specs=(tokens, tokens, tokens, P(DP, SEQ), tokens, rows, rows, rows, rows, rows),
        out_specs=(tokens, rows, rows, rows, rows, rows),
        check_vma=False,
    )
```

```python
import jax
import jax.numpy as jnp
from jax import lax
from jax.experimental import pallas as pl
from jax.experimental.pallas import tpu as pltpu
from jax.sharding import Mesh
from jax.sharding import PartitionSpec as P

QW = 2048
DO = 2304
GROUP = 128
TILE = 256
BLOCKS = 8
NOTE = 16
WIDE = 768
SEQ = ("seq_0", "seq_1")
DP = ("dp_0", "dp_1", "dp_2")
DP_SEQ = ("dp_0", "dp_1", "dp_2", "seq_0", "seq_1")
LOG2E = 1.4426950408889634
VMEM_LIMIT = 60 * 1024 * 1024

score_scale = 144.0 ** (-0.5)
soft_cap = 50.0
beta_first = 0.9
beta_second = 0.95
learn_rate = 0.001
decay_rate = 0.1

F32 = jnp.float32
BF16 = jnp.bfloat16


def params(*semantics):
    return pltpu.CompilerParams(
        vmem_limit_bytes=VMEM_LIMIT,
        dimension_semantics=semantics or None,
    )


def restored(entries):
    wide = entries.astype(F32)
    scale = (jnp.max(jnp.abs(wide), axis=-1, keepdims=True) + 1e-06).astype(BF16).astype(F32)
    coded = (wide / scale).astype(BF16).astype(F32)
    return (coded * scale).astype(BF16)


def pack_kernel(q_ref, k_ref, v_ref, seg_ref, out_ref):
    out_ref[0, :TILE, 0:256] = q_ref[...]
    out_ref[0, :TILE, 256:384] = restored(k_ref[...])
    out_ref[0, :TILE, 384:512] = restored(v_ref[...])
    seg = seg_ref[...]
    below_1 = jnp.sum((seg < 1).astype(F32), axis=-1, keepdims=True)
    below_2 = jnp.sum((seg < 2).astype(F32), axis=-1, keepdims=True)
    out_ref[0, TILE:, 0:256] = jnp.broadcast_to(below_1, (NOTE, 256)).astype(BF16)
    out_ref[0, TILE:, 256:512] = jnp.broadcast_to(below_2, (NOTE, 256)).astype(BF16)


def pack(q, k, v, seg):
    return pl.pallas_call(
        pack_kernel,
        grid=(BLOCKS,),
        in_specs=[
            pl.BlockSpec((TILE, 256), lambda h: (0, h)),
            pl.BlockSpec((TILE, 128), lambda h: (0, h)),
            pl.BlockSpec((TILE, 128), lambda h: (0, h)),
            pl.BlockSpec((1, TILE), lambda h: (0, 0)),
        ],
        out_specs=pl.BlockSpec((1, TILE + NOTE, 512), lambda h: (h, 0, 0)),
        out_shape=jax.ShapeDtypeStruct((BLOCKS, TILE + NOTE, 512), BF16),
        compiler_params=params("arbitrary"),
        name="pack",
    )(q, k, v, seg)


def attend_kernel(in_ref, out_ref, acc, total):
    notes = in_ref[:, TILE : TILE + 8, :].astype(F32).sum(axis=0)
    first_of_1 = jnp.max(notes[:, 0:128]).astype(jnp.int32)
    first_of_2 = jnp.max(notes[:, 256:384]).astype(jnp.int32)

    def first_seen(place):
        return jnp.where(
            place < first_of_1, 0, jnp.where(place < first_of_2, first_of_1, first_of_2)
        )

    key_row = lax.broadcasted_iota(jnp.int32, (TILE, 2 * TILE), 0)
    lane = lax.broadcasted_iota(jnp.int32, (1, 2 * TILE), 1)
    query_col = jnp.where(lane < TILE, lane, lane - TILE)

    for i in range(BLOCKS):
        query = jnp.concatenate([in_ref[i, :TILE, 0:128], in_ref[i, :TILE, 128:256]], axis=0)
        start_row = first_seen(i * TILE + query_col)
        start_low = first_seen(jnp.int32(i * TILE))
        start_high = first_seen(jnp.int32(i * TILE + TILE - 1))
        acc[...] = jnp.zeros_like(acc)
        total[...] = jnp.zeros_like(total)

        def step(j, mask, query=query):
            key = in_ref[j, :TILE, 256:384]
            value = in_ref[j, :TILE, 384:512]
            scores = lax.dot_general(
                key, query, (((1,), (1,)), ((), ())), preferred_element_type=F32
            )
            capped = jnp.tanh(scores * (score_scale / soft_cap))
            weights = jnp.exp2(capped * (soft_cap * LOG2E))
            if mask is not None:
                weights = jnp.where(mask, weights, 0.0)
            total[...] += weights.reshape(TILE // 8, 8, 2 * TILE).sum(axis=0)
            acc[...] += lax.dot_general(
                value, weights.astype(BF16), (((0,), (0,)), ((), ())), preferred_element_type=F32
            )

        low = start_low // TILE
        clear = jnp.minimum((start_high + TILE - 1) // TILE, i)

        @pl.loop(low, clear)
        def _(j):
            step(j, key_row + j * TILE >= start_row)

        @pl.loop(clear, i)
        def _(j):
            step(j, None)

        step(i, (key_row <= query_col) & (key_row + i * TILE >= start_row))

        attended = (acc[...] / jnp.sum(total[...], axis=0, keepdims=True)).astype(BF16)
        for x in range(4):
            for c in range(2):
                out_ref[(x * 2 + c) * BLOCKS + i] = attended[
                    x * 32 : (x + 1) * 32, c * TILE : (c + 1) * TILE
                ]


def attend(packed):
    return pl.pallas_call(
        attend_kernel,
        out_shape=jax.ShapeDtypeStruct((64, 32, TILE), BF16),
        in_specs=[pl.BlockSpec(memory_space=pltpu.VMEM)],
        out_specs=pl.BlockSpec(memory_space=pltpu.VMEM),
        scratch_shapes=[pltpu.VMEM((128, 2 * TILE), F32), pltpu.VMEM((8, 2 * TILE), F32)],
        compiler_params=params(),
        name="attend",
    )(packed)


def gradient_kernel(c_ref, att_ref, own_ref, other_ref, out_ref, left):
    @pl.when(pl.program_id(0) == 0)
    def _():
        for core in range(2):
            mine = c_ref[0] if core == 0 else 1 - c_ref[0]
            for x in range(4):
                left[core, :, x * TILE : (x + 1) * TILE] = att_ref[x * 2 + mine]

    low = (
        jnp.dot(left[0], own_ref[...], preferred_element_type=F32)
        + jnp.dot(left[1], other_ref[...], preferred_element_type=F32)
    ).astype(BF16)
    for fx in range(4):
        for fy in range(2):
            for fh in range(2):
                row = ((fx * 2 + fy) * 2 + fh) * 16
                out_ref[(fy * 4 + fx) * 2 + fh] = low[row : row + 16]


def gradient_rows(core, att, own, other):
    return pl.pallas_call(
        gradient_kernel,
        grid_spec=pltpu.PrefetchScalarGridSpec(
            num_scalar_prefetch=1,
            grid=(DO // WIDE,),
            in_specs=[
                pl.BlockSpec((8, 256, TILE), lambda n, c: (0, 0, 0)),
                pl.BlockSpec((1024, WIDE), lambda n, c: (0, n)),
                pl.BlockSpec((1024, WIDE), lambda n, c: (0, n)),
            ],
            out_specs=pl.BlockSpec((16, 16, WIDE), lambda n, c: (0, 0, n)),
            scratch_shapes=[pltpu.VMEM((2, 256, 1024), BF16)],
        ),
        out_shape=jax.ShapeDtypeStruct((16, 16, DO), BF16),
        compiler_params=params("arbitrary"),
        cost_estimate=pl.CostEstimate(
            flops=2 * 256 * 2048 * DO, bytes_accessed=12_000_000, transcendentals=0
        ),
        name="gradient_rows",
    )(core, att, own, other)


def project_kernel(c_ref, att_ref, own_ref, other_ref, out_ref, left):
    @pl.when(pl.program_id(0) == 0)
    def _():
        for core in range(2):
            mine = c_ref[0] if core == 0 else 1 - c_ref[0]
            for z in range(4):
                left[core, :, z * TILE : (z + 1) * TILE] = att_ref[z * 2 + mine].T

    out_ref[0] = (
        jnp.dot(left[0], own_ref[...], preferred_element_type=F32)
        + jnp.dot(left[1], other_ref[...], preferred_element_type=F32)
    ).astype(BF16)


def project(core, att, own, other):
    return pl.pallas_call(
        project_kernel,
        grid_spec=pltpu.PrefetchScalarGridSpec(
            num_scalar_prefetch=1,
            grid=(DO // WIDE,),
            in_specs=[
                pl.BlockSpec((8, 256, TILE), lambda n, c: (0, 0, 0)),
                pl.BlockSpec((1024, WIDE), lambda n, c: (0, n)),
                pl.BlockSpec((1024, WIDE), lambda n, c: (0, n)),
            ],
            out_specs=pl.BlockSpec((1, TILE, WIDE), lambda n, c: (0, 0, n)),
            scratch_shapes=[pltpu.VMEM((2, TILE, 1024), BF16)],
        ),
        out_shape=jax.ShapeDtypeStruct((1, TILE, DO), BF16),
        compiler_params=params("arbitrary"),
        cost_estimate=pl.CostEstimate(
            flops=2 * 256 * 2048 * DO, bytes_accessed=12_000_000, transcendentals=0
        ),
        name="project",
    )(core, att, own, other)


def total_kernel(parts_ref, grad_ref, squares_ref):
    total = parts_ref[0].astype(F32)
    for k in range(1, 16):
        total += parts_ref[k].astype(F32)
    grad_ref[...] = total
    squares = jnp.sum(total * total)
    squares_ref[...] = jnp.broadcast_to(squares, squares_ref.shape)


def total_rows(parts):
    return pl.pallas_call(
        total_kernel,
        out_shape=(
            jax.ShapeDtypeStruct((16, DO), F32),
            jax.ShapeDtypeStruct((128, 1, 128), F32),
        ),
        compiler_params=params(),
        name="total_rows",
    )(parts)


def adam_kernel(
    grad_ref, squares_ref, weight_ref, first_ref, fscale_ref, second_ref, sscale_ref,
    new_weight_ref, new_first_ref, new_fscale_ref, new_second_ref, new_sscale_ref,
):
    sum_squares = jnp.sum(squares_ref[:, 0, :]) * (1.0 / 128.0)
    rms = jnp.sqrt(jnp.full((16, GROUP), sum_squares * (1.0 / (QW * DO)) + 1e-06, F32))
    shrink = jnp.minimum(1.0, 1.0 / rms)

    def decode(coded, scale):
        magnitude = scale * jnp.sqrt(jnp.abs(coded))
        return jnp.where(coded < 0.0, -magnitude, magnitude)

    def encode(x):
        scale = jnp.max(jnp.abs(x), axis=-1, keepdims=True) + 1e-06
        return (x * jnp.abs(x) / (scale * scale)).astype(BF16), scale

    fscales, sscales = [], []
    for g in range(DO // GROUP):
        at = slice(g * GROUP, (g + 1) * GROUP)
        clipped = grad_ref[:, at] * shrink
        first_old = decode(first_ref[:, at].astype(F32), fscale_ref[:, g : g + 1])
        second_old = decode(second_ref[:, at].astype(F32), sscale_ref[:, g : g + 1])
        first = beta_first * first_old + (1.0 - beta_first) * clipped
        second = beta_second * second_old + (1.0 - beta_second) * clipped * clipped
        weight = weight_ref[:, at]
        new_weight_ref[:, at] = weight - learn_rate * (
            first / (jnp.sqrt(second) + 1e-08) + decay_rate * weight
        )
        new_first_ref[:, at], scale = encode(first)
        fscales.append(scale)
        new_second_ref[:, at], scale = encode(second)
        sscales.append(scale)
    new_fscale_ref[...] = jnp.concatenate(fscales, axis=1)
    new_sscale_ref[...] = jnp.concatenate(sscales, axis=1)


def adam(grad, squares, weight, first, fscale, second, sscale):
    return pl.pallas_call(
        adam_kernel,
        out_shape=tuple(
            jax.ShapeDtypeStruct(a.shape, a.dtype) for a in (weight, first, fscale, second, sscale)
        ),
        compiler_params=params(),
        name="adam",
    )(grad, squares, weight, first, fscale, second, sscale)


def shift(x, axis, by):
    peers = lax.axis_size(axis)
    return lax.ppermute(x, axis, [(i, (i + by) % peers) for i in range(peers)])


def sent_to_all(x, axes):
    peers = lax.axis_size(axes)
    return lax.all_to_all(jnp.broadcast_to(x[None], (peers, *x.shape)), axes, 0, 0, tiled=True)


def local(
    queries, keys, values, segments, cotangent, weight,
    first_moment, first_scale, second_moment, second_scale,
):
    core = lax.axis_index("dp_2").astype(jnp.int32)[None]

    packed = pack(queries[0], keys[0], values[0], segments)
    arrived = lax.all_to_all(packed, SEQ, 0, 0, tiled=True)

    cots = sent_to_all(cotangent[0], "dp_0").reshape(1024, DO)
    other_cots = shift(cots, "dp_2", 1)

    rows = sent_to_all(weight.astype(BF16), ("dp_0", "dp_1", "seq_1")).reshape(256, DO)
    rows = sent_to_all(rows, "seq_0").reshape(1024, DO)
    other_rows = shift(rows, "dp_2", 1)

    attended = attend(arrived)
    columns = lax.all_to_all(
        attended, ("dp_0", "dp_2", "seq_0", "seq_1"), 0, 0, tiled=True
    ).reshape(8, 256, TILE)
    partial = gradient_rows(core, columns, cots, other_cots)
    parts = lax.all_to_all(partial, ("dp_1", "seq_0", "seq_1"), 0, 0, tiled=True)
    grad, squares = total_rows(parts)
    grad = lax.ppermute(
        grad, ("dp_0", "seq_0"), [(x * 4 + z, z * 4 + x) for x in range(4) for z in range(4)]
    )
    squares = lax.all_to_all(squares, DP_SEQ, 0, 0, tiled=True)
    new_weight, new_first, new_fscale, new_second, new_sscale = adam(
        grad, squares, weight, first_moment, first_scale, second_moment, second_scale
    )
    own = lax.all_to_all(columns, ("dp_0", "dp_2"), 0, 0, tiled=True)
    layer_out = project(core, own, rows, other_rows)
    return (layer_out, new_weight, new_first, new_fscale, new_second, new_sscale)


def solution(mesh):
    finer = Mesh(mesh.devices.reshape(4, 2, 2, 4, 2), DP_SEQ)
    tokens = P(DP, SEQ, None)
    rows = P(DP_SEQ, None)
    return jax.shard_map(
        local,
        mesh=finer,
        in_specs=(tokens, tokens, tokens, P(DP, SEQ), tokens, rows, rows, rows, rows, rows),
        out_specs=(tokens, rows, rows, rows, rows, rows),
        check_vma=False,
    )
```

```python
import jax
import jax.numpy as jnp
from jax import lax
from jax.experimental import pallas as pl
from jax.experimental.pallas import tpu as pltpu
from jax.sharding import Mesh
from jax.sharding import PartitionSpec as P

QW = 2048
DO = 2304
GROUP = 128
TILE = 256
BLOCKS = 8
NOTE = 16
WIDE = 768
ORDER = (0, 1, 3, 2)
SEQ = ("seq_0", "seq_1")
DP = ("dp_0", "dp_1", "dp_2")
DP_SEQ = ("dp_0", "dp_1", "dp_2", "seq_0", "seq_1")
LOG2E = 1.4426950408889634
VMEM_LIMIT = 60 * 1024 * 1024

score_scale = 144.0 ** (-0.5)
soft_cap = 50.0
beta_first = 0.9
beta_second = 0.95
learn_rate = 0.001
decay_rate = 0.1

F32 = jnp.float32
BF16 = jnp.bfloat16


def params(*semantics):
    return pltpu.CompilerParams(
        vmem_limit_bytes=VMEM_LIMIT,
        dimension_semantics=semantics or None,
    )


def restored(entries):
    wide = entries.astype(F32)
    scale = (jnp.max(jnp.abs(wide), axis=-1, keepdims=True) + 1e-06).astype(BF16).astype(F32)
    coded = (wide / scale).astype(BF16).astype(F32)
    return (coded * scale).astype(BF16)


def pack_kernel(q_ref, k_ref, v_ref, seg_ref, out_ref):
    seg = seg_ref[...]
    below_1 = jnp.sum((seg < 1).astype(F32), axis=-1, keepdims=True)
    below_2 = jnp.sum((seg < 2).astype(F32), axis=-1, keepdims=True)
    notes = jnp.concatenate(
        [jnp.broadcast_to(b, (NOTE, 256)) for b in (below_1, below_2)], axis=1
    ).astype(BF16)
    for h in range(BLOCKS):
        out_ref[h, :TILE, 0:256] = q_ref[:, h * 256 : (h + 1) * 256]
        out_ref[h, :TILE, 256:384] = restored(k_ref[:, h * 128 : (h + 1) * 128])
        out_ref[h, :TILE, 384:512] = restored(v_ref[:, h * 128 : (h + 1) * 128])
        out_ref[h, TILE:, :] = notes


def pack(q, k, v, seg):
    return pl.pallas_call(
        pack_kernel,
        out_shape=jax.ShapeDtypeStruct((BLOCKS, TILE + NOTE, 512), BF16),
        compiler_params=params(),
        cost_estimate=pl.CostEstimate(flops=0, bytes_accessed=6_000_000, transcendentals=0),
        name="pack",
    )(q, k, v, seg)


def attend_kernel(in_ref, out_ref, acc, total):
    notes = in_ref[:, TILE : TILE + 8, :].astype(F32).sum(axis=0)
    first_of_1 = jnp.max(notes[:, 0:128]).astype(jnp.int32)
    first_of_2 = jnp.max(notes[:, 256:384]).astype(jnp.int32)

    def first_seen(place):
        return jnp.where(
            place < first_of_1, 0, jnp.where(place < first_of_2, first_of_1, first_of_2)
        )

    key_row = lax.broadcasted_iota(jnp.int32, (TILE, 2 * TILE), 0)
    lane = lax.broadcasted_iota(jnp.int32, (1, 2 * TILE), 1)
    query_col = jnp.where(lane < TILE, lane, lane - TILE)

    for i in range(BLOCKS):
        query = jnp.concatenate([in_ref[i, :TILE, 0:128], in_ref[i, :TILE, 128:256]], axis=0)
        start_row = first_seen(i * TILE + query_col)
        start_low = first_seen(jnp.int32(i * TILE))
        start_high = first_seen(jnp.int32(i * TILE + TILE - 1))
        acc[...] = jnp.zeros_like(acc)
        total[...] = jnp.zeros_like(total)

        def step(j, mask, query=query):
            key = in_ref[j, :TILE, 256:384]
            value = in_ref[j, :TILE, 384:512]
            scores = lax.dot_general(
                key, query, (((1,), (1,)), ((), ())), preferred_element_type=F32
            )
            capped = jnp.tanh(scores * (score_scale / soft_cap))
            weights = jnp.exp2(capped * (soft_cap * LOG2E))
            if mask is not None:
                weights = jnp.where(mask, weights, 0.0)
            total[...] += weights.reshape(TILE // 8, 8, 2 * TILE).sum(axis=0)
            acc[...] += lax.dot_general(
                value, weights.astype(BF16), (((0,), (0,)), ((), ())), preferred_element_type=F32
            )

        low = start_low // TILE
        clear = jnp.minimum((start_high + TILE - 1) // TILE, i)

        @pl.loop(low, clear)
        def _(j):
            step(j, key_row + j * TILE >= start_row)

        @pl.loop(clear, i)
        def _(j):
            step(j, None)

        step(i, (key_row <= query_col) & (key_row + i * TILE >= start_row))

        attended = (acc[...] / jnp.sum(total[...], axis=0, keepdims=True)).astype(BF16)
        for c in range(2):
            out_ref[i, c * 128 : (c + 1) * 128] = attended[:, c * TILE : (c + 1) * TILE]


def attend(packed):
    return pl.pallas_call(
        attend_kernel,
        out_shape=jax.ShapeDtypeStruct((BLOCKS, 256, TILE), BF16),
        in_specs=[pl.BlockSpec(memory_space=pltpu.VMEM)],
        out_specs=pl.BlockSpec(memory_space=pltpu.VMEM),
        scratch_shapes=[pltpu.VMEM((128, 2 * TILE), F32), pltpu.VMEM((8, 2 * TILE), F32)],
        compiler_params=params(),
        cost_estimate=pl.CostEstimate(
            flops=10_000_000_000, bytes_accessed=4_000_000, transcendentals=0
        ),
        name="attend",
    )(packed)


def gradient_kernel(me_ref, att_ref, *refs):
    cots, out_ref, left = refs[:10], refs[10], refs[11]

    @pl.when(pl.program_id(0) == 0)
    def _():
        for core in range(2):
            mine = me_ref[2] if core == 0 else 1 - me_ref[2]
            for k, back in enumerate(ORDER):
                x = lax.rem(me_ref[0] + 4 - back, 4)
                low = core * 1024 + k * TILE
                left[:, low : low + TILE] = att_ref[x * 2 + mine]

    right = jnp.concatenate([r[...] for r in cots], axis=0)
    low = jnp.dot(left[...], right, preferred_element_type=F32).astype(BF16)
    out_ref[...] = low.reshape(16, 16, WIDE)


def project_kernel(me_ref, att_ref, *refs):
    rows, out_ref, left = refs[:10], refs[10], refs[11]
    x, c, z = me_ref[0], me_ref[2], me_ref[3]
    y = me_ref[4] * 2 + me_ref[1]

    @pl.when(pl.program_id(0) == 0)
    def _():
        for core in range(2):
            row_c = c if core == 0 else 1 - c
            for k, back in enumerate(ORDER):
                row_x = lax.rem(x + 4 - back, 4)
                blocks = []
                for back_z in range(4):
                    row_z = lax.rem(z + 4 - back_z, 4)
                    for back_y in range(4):
                        row_y = lax.rem(y + 4 - back_y, 4)
                        low, high = lax.rem(row_y, 2), row_y // 2
                        blocks.append(att_ref[row_x * 2 + low, row_c * 8 + row_z * 2 + high])
                at = core * 1024 + k * TILE
                left[:, at : at + TILE] = jnp.concatenate(blocks, axis=0).T

    right = jnp.concatenate([r[...] for r in rows], axis=0)
    out_ref[0] = jnp.dot(left[...], right, preferred_element_type=F32).astype(BF16)


def over_columns(kernel, me, fixed, moving, out_block, out_shape, name, flops):
    return pl.pallas_call(
        kernel,
        grid_spec=pltpu.PrefetchScalarGridSpec(
            num_scalar_prefetch=1,
            grid=(DO // WIDE,),
            in_specs=[pl.BlockSpec(a.shape, lambda n, me, d=a.ndim: (0,) * d) for a in fixed]
            + [pl.BlockSpec((a.shape[0], WIDE), lambda n, me: (0, n)) for a in moving],
            out_specs=pl.BlockSpec(out_block, lambda n, me: (0, 0, n)),
            scratch_shapes=[pltpu.VMEM((TILE, 2048), BF16)],
        ),
        out_shape=jax.ShapeDtypeStruct(out_shape, BF16),
        compiler_params=params("arbitrary"),
        cost_estimate=pl.CostEstimate(flops=flops, bytes_accessed=flops // 200, transcendentals=0),
        name=name,
    )(me, *fixed, *moving)


def total_kernel(parts_ref, grad_ref, squares_ref):
    total = parts_ref[0].astype(F32)
    for k in range(1, 16):
        total += parts_ref[k].astype(F32)
    grad_ref[...] = total
    squares = jnp.sum(total * total)
    squares_ref[...] = jnp.broadcast_to(squares, squares_ref.shape)


def total_rows(parts):
    return pl.pallas_call(
        total_kernel,
        out_shape=(
            jax.ShapeDtypeStruct((16, DO), F32),
            jax.ShapeDtypeStruct((128, 1, 128), F32),
        ),
        compiler_params=params(),
        name="total_rows",
    )(parts)


def adam_kernel(
    grad_ref, squares_ref, weight_ref, first_ref, fscale_ref, second_ref, sscale_ref,
    new_weight_ref, new_first_ref, new_fscale_ref, new_second_ref, new_sscale_ref,
):
    sum_squares = jnp.sum(squares_ref[:, 0, :]) * (1.0 / 128.0)
    rms = jnp.sqrt(jnp.full((16, GROUP), sum_squares * (1.0 / (QW * DO)) + 1e-06, F32))
    shrink = jnp.minimum(1.0, 1.0 / rms)

    def decode(coded, scale):
        magnitude = scale * jnp.sqrt(jnp.abs(coded))
        return jnp.where(coded < 0.0, -magnitude, magnitude)

    def encode(x):
        scale = jnp.max(jnp.abs(x), axis=-1, keepdims=True) + 1e-06
        return (x * jnp.abs(x) / (scale * scale)).astype(BF16), scale

    fscales, sscales = [], []
    for g in range(DO // GROUP):
        at = slice(g * GROUP, (g + 1) * GROUP)
        clipped = grad_ref[:, at] * shrink
        first_old = decode(first_ref[:, at].astype(F32), fscale_ref[:, g : g + 1])
        second_old = decode(second_ref[:, at].astype(F32), sscale_ref[:, g : g + 1])
        first = beta_first * first_old + (1.0 - beta_first) * clipped
        second = beta_second * second_old + (1.0 - beta_second) * clipped * clipped
        weight = weight_ref[:, at]
        new_weight_ref[:, at] = weight - learn_rate * (
            first / (jnp.sqrt(second) + 1e-08) + decay_rate * weight
        )
        new_first_ref[:, at], scale = encode(first)
        fscales.append(scale)
        new_second_ref[:, at], scale = encode(second)
        sscales.append(scale)
    new_fscale_ref[...] = jnp.concatenate(fscales, axis=1)
    new_sscale_ref[...] = jnp.concatenate(sscales, axis=1)


def adam(grad, squares, weight, first, fscale, second, sscale):
    return pl.pallas_call(
        adam_kernel,
        out_shape=tuple(
            jax.ShapeDtypeStruct(a.shape, a.dtype) for a in (weight, first, fscale, second, sscale)
        ),
        compiler_params=params(),
        name="adam",
    )(grad, squares, weight, first, fscale, second, sscale)


def shift(x, axis, by):
    peers = lax.axis_size(axis)
    return lax.ppermute(x, axis, [(i, (i + by) % peers) for i in range(peers)])


def after(x, earlier):
    return lax.optimization_barrier((x, earlier))[0]


def from_ring(mine):
    half = mine.shape[0] // 2
    left, right = shift(mine, "dp_0", 1), shift(mine, "dp_0", -1)
    top, bottom = shift(left[:half], "dp_0", 1), shift(right[half:], "dp_0", -1)
    return [mine, left, right, top, bottom]


def from_partner(arrays):
    return [shift(a, "dp_2", 1) for a in arrays]


def shift_y(x, by):
    pairs = []
    for y in range(4):
        to = (y + by) % 4
        pairs.append(((y % 2) * 2 + y // 2, (to % 2) * 2 + to // 2))
    return lax.ppermute(x, ("dp_1", "seq_1"), pairs)


def local(
    queries, keys, values, segments, cotangent, weight,
    first_moment, first_scale, second_moment, second_scale,
):
    me = jnp.stack([lax.axis_index(a) for a in DP_SEQ]).astype(jnp.int32)

    packed = pack(queries[0], keys[0], values[0], segments)
    arrived = lax.all_to_all(packed, SEQ, 0, 0, tiled=True)
    cots = from_ring(cotangent[0])

    attended = attend(arrived)
    own = lax.all_to_all(attended, SEQ, 0, 0, tiled=True)
    cots = cots + from_partner([after(a, attended) for a in cots])
    rows = after(weight.astype(BF16), attended)
    rows = jnp.concatenate([rows] + [shift_y(rows, k) for k in (1, 2, 3)], axis=0)

    columns = lax.all_to_all(own, ("dp_0", "dp_2"), 0, 0, tiled=True)
    rows = after(rows, own)
    rows = jnp.concatenate([rows] + [shift(rows, "seq_0", k) for k in (1, 2, 3)], axis=0)

    partial = over_columns(
        gradient_kernel, me, [columns], cots, (16, 16, WIDE), (16, 16, DO), "gradient_rows",
        2 * 256 * 2048 * DO,
    )
    rows = from_ring(after(rows, columns))
    parts = lax.all_to_all(partial, ("dp_1", "seq_0", "seq_1"), 0, 0, tiled=True)

    sums, squares = total_rows(parts)
    grad = lax.ppermute(sums, ("dp_1", "dp_2"), [(0, 0), (1, 2), (2, 1), (3, 3)])
    squares = lax.all_to_all(squares, DP_SEQ, 0, 0, tiled=True)
    rows = rows + from_partner(
        [after(a, partial) for a in rows[:3]] + [after(a, sums) for a in rows[3:]]
    )
    layer_out = over_columns(
        project_kernel, me, [own.reshape(8, 16, 16, TILE)], rows,
        (1, TILE, WIDE), (1, TILE, DO), "project", 1000,
    )
    new_weight, new_first, new_fscale, new_second, new_sscale = adam(
        after(grad, layer_out), squares, weight,
        first_moment, first_scale, second_moment, second_scale,
    )
    return (layer_out, new_weight, new_first, new_fscale, new_second, new_sscale)


def solution(mesh):
    finer = Mesh(mesh.devices.reshape(4, 2, 2, 4, 2), DP_SEQ)
    tokens = P(DP, SEQ, None)
    rows = P(DP_SEQ, None)
    return jax.shard_map(
        local,
        mesh=finer,
        in_specs=(tokens, tokens, tokens, P(DP, SEQ), tokens, rows, rows, rows, rows, rows),
        out_specs=(tokens, rows, rows, rows, rows, rows),
        check_vma=False,
    )
```

```python
import jax
import jax.numpy as jnp
from jax import lax
from jax.experimental import pallas as pl
from jax.experimental.pallas import tpu as pltpu
from jax.sharding import Mesh
from jax.sharding import PartitionSpec as P

QW = 2048
DO = 2304
GROUP = 128
TILE = 256
BLOCKS = 8
NOTE = 16
WIDE = 1152
ORDER = (0, 1, 3, 2)
SEQ = ("seq_0", "seq_1")
DP = ("dp_0", "dp_1", "dp_2")
DP_SEQ = ("dp_0", "dp_1", "dp_2", "seq_0", "seq_1")
LOG2E = 1.4426950408889634
VMEM_LIMIT = 60 * 1024 * 1024

score_scale = 144.0 ** (-0.5)
soft_cap = 50.0
beta_first = 0.9
beta_second = 0.95
learn_rate = 0.001
decay_rate = 0.1

F32 = jnp.float32
BF16 = jnp.bfloat16


def params(*semantics):
    return pltpu.CompilerParams(
        vmem_limit_bytes=VMEM_LIMIT,
        dimension_semantics=semantics or None,
    )


def restored(entries):
    wide = entries.astype(F32)
    scale = (jnp.max(jnp.abs(wide), axis=-1, keepdims=True) + 1e-06).astype(BF16).astype(F32)
    coded = (wide / scale).astype(BF16).astype(F32)
    return (coded * scale).astype(BF16)


def pack_kernel(q_ref, k_ref, v_ref, seg_ref, out_ref):
    seg = seg_ref[...]
    below_1 = jnp.sum((seg < 1).astype(F32), axis=-1, keepdims=True)
    below_2 = jnp.sum((seg < 2).astype(F32), axis=-1, keepdims=True)
    notes = jnp.concatenate(
        [jnp.broadcast_to(b, (NOTE, 256)) for b in (below_1, below_2)], axis=1
    ).astype(BF16)
    for h in range(BLOCKS):
        out_ref[h, :TILE, 0:256] = q_ref[:, h * 256 : (h + 1) * 256]
        out_ref[h, :TILE, 256:384] = restored(k_ref[:, h * 128 : (h + 1) * 128])
        out_ref[h, :TILE, 384:512] = restored(v_ref[:, h * 128 : (h + 1) * 128])
        out_ref[h, TILE:, :] = notes


def pack(q, k, v, seg):
    return pl.pallas_call(
        pack_kernel,
        out_shape=jax.ShapeDtypeStruct((BLOCKS, TILE + NOTE, 512), BF16),
        compiler_params=params(),
        cost_estimate=pl.CostEstimate(flops=0, bytes_accessed=6_000_000, transcendentals=0),
        name="pack",
    )(q, k, v, seg)


def attend_kernel(in_ref, out_ref):
    notes = in_ref[:, TILE : TILE + 8, :].astype(F32).sum(axis=0)
    first_of_1 = jnp.max(notes[:, 0:128]).astype(jnp.int32)
    first_of_2 = jnp.max(notes[:, 256:384]).astype(jnp.int32)

    def first_seen(place):
        return jnp.where(
            place < first_of_1, 0, jnp.where(place < first_of_2, first_of_1, first_of_2)
        )

    def tile(i, low):
        lane = lax.broadcasted_iota(jnp.int32, (1, 2 * TILE), 1)
        place = jnp.where(lane < TILE, lane, lane - TILE) + i * TILE
        seen = range(low, i + 1)
        query = jnp.concatenate([in_ref[i, :TILE, 0:128], in_ref[i, :TILE, 128:256]], axis=0)
        key = jnp.concatenate([in_ref[j, :TILE, 256:384] for j in seen], axis=0)
        value = jnp.concatenate([in_ref[j, :TILE, 384:512] for j in seen], axis=0)
        key_place = lax.broadcasted_iota(jnp.int32, (len(seen) * TILE, 2 * TILE), 0) + low * TILE
        scores = lax.dot_general(key, query, (((1,), (1,)), ((), ())), preferred_element_type=F32)
        capped = jnp.tanh(scores * (score_scale / soft_cap))
        weights = jnp.exp2(capped * (soft_cap * LOG2E))
        weights = jnp.where((key_place >= first_seen(place)) & (key_place <= place), weights, 0.0)
        total = jnp.sum(weights, axis=0, keepdims=True)
        mixed = lax.dot_general(
            value, weights.astype(BF16), (((0,), (0,)), ((), ())), preferred_element_type=F32
        )
        attended = (mixed / total).astype(BF16)
        for c in range(2):
            out_ref[i, c * 128 : (c + 1) * 128] = attended[:, c * TILE : (c + 1) * TILE]

    for i in range(BLOCKS):
        first = first_seen(jnp.int32(i * TILE)) // TILE
        for low in range(max(0, i - 5), i + 1):
            pl.when(first == low)(lambda i=i, low=low: tile(i, low))


def attend(packed):
    return pl.pallas_call(
        attend_kernel,
        out_shape=jax.ShapeDtypeStruct((BLOCKS, 256, TILE), BF16),
        in_specs=[pl.BlockSpec(memory_space=pltpu.VMEM)],
        out_specs=pl.BlockSpec(memory_space=pltpu.VMEM),
        compiler_params=params(),
        cost_estimate=pl.CostEstimate(
            flops=10_000_000_000, bytes_accessed=4_000_000, transcendentals=0
        ),
        name="attend",
    )(packed)


def gradient_kernel(me_ref, att_ref, *refs):
    cots, out_ref, left = refs[:10], refs[10], refs[11]

    @pl.when(pl.program_id(0) == 0)
    def _():
        for core in range(2):
            mine = me_ref[2] if core == 0 else 1 - me_ref[2]
            for k, back in enumerate(ORDER):
                x = lax.rem(me_ref[0] + 4 - back, 4)
                low = core * 1024 + k * TILE
                left[:, low : low + TILE] = att_ref[x * 2 + mine]

    right = jnp.concatenate([r[...] for r in cots], axis=0)
    low = jnp.dot(left[...], right, preferred_element_type=F32).astype(BF16)
    out_ref[...] = low.reshape(16, 16, WIDE)


def project_kernel(me_ref, att_ref, *refs):
    rows, out_ref, left = refs[:16], refs[16], refs[17]
    x, c, z = me_ref[0], me_ref[2], me_ref[3]
    y = me_ref[4] * 2 + me_ref[1]

    @pl.when(pl.program_id(0) == 0)
    def _():
        for core in range(2):
            row_c = c if core == 0 else 1 - c
            for k, back in enumerate(ORDER):
                row_x = lax.rem(x + 4 - back, 4)
                blocks = []
                for back_z in range(4):
                    row_z = lax.rem(z + 4 - back_z, 4)
                    for back_y in range(4):
                        row_y = lax.rem(y + 4 - back_y, 4)
                        low, high = lax.rem(row_y, 2), row_y // 2
                        blocks.append(att_ref[row_x * 2 + low, row_c * 8 + row_z * 2 + high])
                at = core * 1024 + k * TILE
                left[:, at : at + TILE] = jnp.concatenate(blocks, axis=0).T

    right = jnp.concatenate([r[...] for r in rows], axis=0)
    out_ref[0] = jnp.dot(left[...], right, preferred_element_type=F32).astype(BF16)


def over_columns(kernel, me, fixed, moving, out_block, out_shape, name, flops):
    return pl.pallas_call(
        kernel,
        grid_spec=pltpu.PrefetchScalarGridSpec(
            num_scalar_prefetch=1,
            grid=(DO // WIDE,),
            in_specs=[pl.BlockSpec(a.shape, lambda n, me, d=a.ndim: (0,) * d) for a in fixed]
            + [pl.BlockSpec((a.shape[0], WIDE), lambda n, me: (0, n)) for a in moving],
            out_specs=pl.BlockSpec(out_block, lambda n, me: (0, 0, n)),
            scratch_shapes=[pltpu.VMEM((TILE, 2048), BF16)],
        ),
        out_shape=jax.ShapeDtypeStruct(out_shape, BF16),
        compiler_params=params("arbitrary"),
        cost_estimate=pl.CostEstimate(flops=flops, bytes_accessed=flops // 200, transcendentals=0),
        name=name,
    )(me, *fixed, *moving)


def total_kernel(parts_ref, grad_ref, squares_ref):
    total = parts_ref[0].astype(F32)
    for k in range(1, 16):
        total += parts_ref[k].astype(F32)
    grad_ref[...] = total
    squares = jnp.sum(total * total)
    squares_ref[...] = jnp.broadcast_to(squares, squares_ref.shape)


def total_rows(parts):
    return pl.pallas_call(
        total_kernel,
        out_shape=(
            jax.ShapeDtypeStruct((16, DO), F32),
            jax.ShapeDtypeStruct((128, 1, 128), F32),
        ),
        compiler_params=params(),
        name="total_rows",
    )(parts)


def adam_kernel(
    grad_ref, squares_ref, weight_ref, first_ref, fscale_ref, second_ref, sscale_ref,
    new_weight_ref, new_first_ref, new_fscale_ref, new_second_ref, new_sscale_ref,
):
    sum_squares = jnp.sum(squares_ref[:, 0, :]) * (1.0 / 128.0)
    rms = jnp.sqrt(jnp.full((16, GROUP), sum_squares * (1.0 / (QW * DO)) + 1e-06, F32))
    shrink = jnp.minimum(1.0, 1.0 / rms)

    def decode(coded, scale):
        magnitude = scale * jnp.sqrt(jnp.abs(coded))
        return jnp.where(coded < 0.0, -magnitude, magnitude)

    def encode(x):
        scale = jnp.max(jnp.abs(x), axis=-1, keepdims=True) + 1e-06
        return (x * jnp.abs(x) / (scale * scale)).astype(BF16), scale

    fscales, sscales = [], []
    for g in range(DO // GROUP):
        at = slice(g * GROUP, (g + 1) * GROUP)
        clipped = grad_ref[:, at] * shrink
        first_old = decode(first_ref[:, at].astype(F32), fscale_ref[:, g : g + 1])
        second_old = decode(second_ref[:, at].astype(F32), sscale_ref[:, g : g + 1])
        first = beta_first * first_old + (1.0 - beta_first) * clipped
        second = beta_second * second_old + (1.0 - beta_second) * clipped * clipped
        weight = weight_ref[:, at]
        new_weight_ref[:, at] = weight - learn_rate * (
            first / (jnp.sqrt(second) + 1e-08) + decay_rate * weight
        )
        new_first_ref[:, at], scale = encode(first)
        fscales.append(scale)
        new_second_ref[:, at], scale = encode(second)
        sscales.append(scale)
    new_fscale_ref[...] = jnp.concatenate(fscales, axis=1)
    new_sscale_ref[...] = jnp.concatenate(sscales, axis=1)


def adam(grad, squares, weight, first, fscale, second, sscale):
    return pl.pallas_call(
        adam_kernel,
        out_shape=tuple(
            jax.ShapeDtypeStruct(a.shape, a.dtype) for a in (weight, first, fscale, second, sscale)
        ),
        compiler_params=params(),
        cost_estimate=pl.CostEstimate(
            flops=30_000_000_000, bytes_accessed=1_000_000, transcendentals=0
        ),
        name="adam",
    )(grad, squares, weight, first, fscale, second, sscale)


def shift(x, axis, by):
    peers = lax.axis_size(axis)
    return lax.ppermute(x, axis, [(i, (i + by) % peers) for i in range(peers)])


def after(x, earlier):
    return lax.optimization_barrier((x, earlier))[0]


def from_ring(mine):
    half = mine.shape[0] // 2
    left, right = shift(mine, "dp_0", 1), shift(mine, "dp_0", -1)
    top, bottom = shift(left[:half], "dp_0", 1), shift(right[half:], "dp_0", -1)
    return [mine, left, right, top, bottom]


def from_partner(arrays):
    return [shift(a, "dp_2", 1) for a in arrays]


def shift_y(x, by):
    pairs = []
    for y in range(4):
        to = (y + by) % 4
        pairs.append(((y % 2) * 2 + y // 2, (to % 2) * 2 + to // 2))
    return lax.ppermute(x, ("dp_1", "seq_1"), pairs)


def local(
    queries, keys, values, segments, cotangent, weight,
    first_moment, first_scale, second_moment, second_scale,
):
    me = jnp.stack([lax.axis_index(a) for a in DP_SEQ]).astype(jnp.int32)

    packed = pack(queries[0], keys[0], values[0], segments)
    arrived = lax.all_to_all(packed, SEQ, 0, 0, tiled=True)
    cots = from_ring(cotangent[0])

    attended = attend(arrived)
    own = lax.all_to_all(attended, SEQ, 0, 0, tiled=True)
    cots = cots + from_partner([after(a, attended) for a in cots])
    rows = after(weight.astype(BF16), attended)
    rows = jnp.concatenate([rows] + [shift_y(rows, k) for k in (1, 2, 3)], axis=0)

    columns = lax.all_to_all(own, ("dp_0", "dp_2"), 0, 0, tiled=True)
    rows = after(rows, own)
    rows = [rows] + [shift(rows, "seq_0", k) for k in (1, 2, 3)]
    top, bottom = jnp.concatenate(rows[:2], axis=0), jnp.concatenate(rows[2:], axis=0)

    partial = over_columns(
        gradient_kernel, me, [columns], cots, (16, 16, WIDE), (16, 16, DO), "gradient_rows",
        2 * 256 * 2048 * DO,
    )
    top, bottom = after(top, columns), after(bottom, columns)
    left_top, right_bottom = shift(top, "dp_0", 1), shift(bottom, "dp_0", -1)
    far_top, far_bottom = shift(left_top, "dp_0", 1), shift(right_bottom, "dp_0", -1)
    left_bottom = shift(after(bottom, partial), "dp_0", 1)
    right_top = shift(after(top, partial), "dp_0", -1)
    rows = [top, bottom, left_top, left_bottom, right_top, right_bottom, far_top, far_bottom]
    parts = lax.all_to_all(partial, ("dp_1", "seq_0", "seq_1"), 0, 0, tiled=True)

    sums, squares = total_rows(parts)
    grad = lax.ppermute(sums, ("dp_1", "dp_2"), [(0, 0), (1, 2), (2, 1), (3, 3)])
    squares = lax.all_to_all(squares, DP_SEQ, 0, 0, tiled=True)
    rows = rows + from_partner(
        [after(a, partial if k in (0, 1, 2, 5) else squares) for k, a in enumerate(rows)]
    )
    layer_out = over_columns(
        project_kernel, me, [own.reshape(8, 16, 16, TILE)], rows,
        (1, TILE, WIDE), (1, TILE, DO), "project", 1000,
    )
    new_weight, new_first, new_fscale, new_second, new_sscale = adam(
        grad, squares, weight,
        first_moment, first_scale, second_moment, second_scale,
    )
    return (layer_out, new_weight, new_first, new_fscale, new_second, new_sscale)


def solution(mesh):
    finer = Mesh(mesh.devices.reshape(4, 2, 2, 4, 2), DP_SEQ)
    tokens = P(DP, SEQ, None)
    rows = P(DP_SEQ, None)
    return jax.shard_map(
        local,
        mesh=finer,
        in_specs=(tokens, tokens, tokens, P(DP, SEQ), tokens, rows, rows, rows, rows, rows),
        out_specs=(tokens, rows, rows, rows, rows, rows),
        check_vma=False,
    )
```

```python
import jax
import jax.numpy as jnp
from jax import lax
from jax.experimental import pallas as pl
from jax.experimental.pallas import tpu as pltpu
from jax.sharding import Mesh
from jax.sharding import PartitionSpec as P

QW = 2048
DO = 2304
GROUP = 128
TILE = 256
BLOCKS = 8
NOTE = 16
WIDE = 1152
ORDER = (0, 1, 3, 2)
SEQ = ("seq_0", "seq_1")
DP = ("dp_0", "dp_1", "dp_2")
DP_SEQ = ("dp_0", "dp_1", "dp_2", "seq_0", "seq_1")
LOG2E = 1.4426950408889634
VMEM_LIMIT = 60 * 1024 * 1024

score_scale = 144.0 ** (-0.5)
soft_cap = 50.0
beta_first = 0.9
beta_second = 0.95
learn_rate = 0.001
decay_rate = 0.1

F32 = jnp.float32
BF16 = jnp.bfloat16


def params(*semantics):
    return pltpu.CompilerParams(
        vmem_limit_bytes=VMEM_LIMIT,
        dimension_semantics=semantics or None,
    )


def restored(entries):
    wide = entries.astype(F32)
    scale = (jnp.max(jnp.abs(wide), axis=-1, keepdims=True) + 1e-06).astype(BF16).astype(F32)
    coded = (wide / scale).astype(BF16).astype(F32)
    return (coded * scale).astype(BF16)


def pack_kernel(q_ref, k_ref, v_ref, seg_ref, out_ref):
    seg = seg_ref[...]
    below_1 = jnp.sum((seg < 1).astype(F32), axis=-1, keepdims=True)
    below_2 = jnp.sum((seg < 2).astype(F32), axis=-1, keepdims=True)
    notes = jnp.concatenate(
        [jnp.broadcast_to(b, (NOTE, 256)) for b in (below_1, below_2)], axis=1
    ).astype(BF16)
    for h in range(BLOCKS):
        out_ref[h, :TILE, 0:256] = q_ref[:, h * 256 : (h + 1) * 256]
        out_ref[h, :TILE, 256:384] = restored(k_ref[:, h * 128 : (h + 1) * 128])
        out_ref[h, :TILE, 384:512] = restored(v_ref[:, h * 128 : (h + 1) * 128])
        out_ref[h, TILE:, :] = notes


def pack(q, k, v, seg):
    return pl.pallas_call(
        pack_kernel,
        out_shape=jax.ShapeDtypeStruct((BLOCKS, TILE + NOTE, 512), BF16),
        compiler_params=params(),
        cost_estimate=pl.CostEstimate(flops=0, bytes_accessed=6_000_000, transcendentals=0),
        name="pack",
    )(q, k, v, seg)


def attend_kernel(in_ref, out_ref):
    notes = in_ref[:, TILE : TILE + 8, :].astype(F32).sum(axis=0)
    first_of_1 = jnp.max(notes[:, 0:128]).astype(jnp.int32)
    first_of_2 = jnp.max(notes[:, 256:384]).astype(jnp.int32)

    def first_seen(place):
        return jnp.where(
            place < first_of_1, 0, jnp.where(place < first_of_2, first_of_1, first_of_2)
        )

    def tile(i, low):
        lane = lax.broadcasted_iota(jnp.int32, (1, 2 * TILE), 1)
        place = jnp.where(lane < TILE, lane, lane - TILE) + i * TILE
        seen = range(low, i + 1)
        query = jnp.concatenate([in_ref[i, :TILE, 0:128], in_ref[i, :TILE, 128:256]], axis=0)
        key = jnp.concatenate([in_ref[j, :TILE, 256:384] for j in seen], axis=0)
        value = jnp.concatenate([in_ref[j, :TILE, 384:512] for j in seen], axis=0)
        key_place = lax.broadcasted_iota(jnp.int32, (len(seen) * TILE, 2 * TILE), 0) + low * TILE
        scores = lax.dot_general(key, query, (((1,), (1,)), ((), ())), preferred_element_type=F32)
        capped = jnp.tanh(scores * (score_scale / soft_cap))
        weights = jnp.exp2(capped * (soft_cap * LOG2E))
        weights = jnp.where((key_place >= first_seen(place)) & (key_place <= place), weights, 0.0)
        total = jnp.sum(weights, axis=0, keepdims=True)
        mixed = lax.dot_general(
            value, weights.astype(BF16), (((0,), (0,)), ((), ())), preferred_element_type=F32
        )
        attended = (mixed / total).astype(BF16)
        for c in range(2):
            out_ref[i, c * 128 : (c + 1) * 128] = attended[:, c * TILE : (c + 1) * TILE]

    for i in range(BLOCKS):
        first = first_seen(jnp.int32(i * TILE)) // TILE
        for low in range(max(0, i - 5), i + 1):
            pl.when(first == low)(lambda i=i, low=low: tile(i, low))


def attend(packed):
    return pl.pallas_call(
        attend_kernel,
        out_shape=jax.ShapeDtypeStruct((BLOCKS, 256, TILE), BF16),
        in_specs=[pl.BlockSpec(memory_space=pltpu.VMEM)],
        out_specs=pl.BlockSpec(memory_space=pltpu.VMEM),
        compiler_params=params(),
        cost_estimate=pl.CostEstimate(
            flops=10_000_000_000, bytes_accessed=4_000_000, transcendentals=0
        ),
        name="attend",
    )(packed)


def gradient_kernel(me_ref, att_ref, *refs):
    cots, out_ref, left = refs[:10], refs[10], refs[11]

    @pl.when(pl.program_id(0) == 0)
    def _():
        for core in range(2):
            mine = me_ref[2] if core == 0 else 1 - me_ref[2]
            for k, back in enumerate(ORDER):
                x = lax.rem(me_ref[0] + 4 - back, 4)
                low = core * 1024 + k * TILE
                left[:, low : low + TILE] = att_ref[x * 2 + mine]

    right = jnp.concatenate([r[...] for r in cots], axis=0)
    low = jnp.dot(left[...], right, preferred_element_type=F32).astype(BF16)
    out_ref[...] = low.reshape(16, 16, WIDE)


def project_kernel(me_ref, att_ref, *refs):
    rows, out_ref, left = refs[:10], refs[10], refs[11]
    x, c, z = me_ref[0], me_ref[2], me_ref[3]
    y = me_ref[4] * 2 + me_ref[1]

    @pl.when(pl.program_id(0) == 0)
    def _():
        for core in range(2):
            row_c = c if core == 0 else 1 - c
            for k, back in enumerate(ORDER):
                row_x = lax.rem(x + 4 - back, 4)
                blocks = []
                for back_z in range(4):
                    row_z = lax.rem(z + 4 - back_z, 4)
                    for back_y in range(4):
                        row_y = lax.rem(y + 4 - back_y, 4)
                        low, high = lax.rem(row_y, 2), row_y // 2
                        blocks.append(att_ref[row_x * 2 + low, row_c * 8 + row_z * 2 + high])
                at = core * 1024 + k * TILE
                left[:, at : at + TILE] = jnp.concatenate(blocks, axis=0).T

    right = jnp.concatenate([r[...] for r in rows], axis=0)
    out_ref[0] = jnp.dot(left[...], right, preferred_element_type=F32).astype(BF16)


def over_columns(kernel, me, fixed, moving, out_block, out_shape, name, flops):
    return pl.pallas_call(
        kernel,
        grid_spec=pltpu.PrefetchScalarGridSpec(
            num_scalar_prefetch=1,
            grid=(DO // WIDE,),
            in_specs=[pl.BlockSpec(a.shape, lambda n, me, d=a.ndim: (0,) * d) for a in fixed]
            + [pl.BlockSpec((a.shape[0], WIDE), lambda n, me: (0, n)) for a in moving],
            out_specs=pl.BlockSpec(out_block, lambda n, me: (0, 0, n)),
            scratch_shapes=[pltpu.VMEM((TILE, 2048), BF16)],
        ),
        out_shape=jax.ShapeDtypeStruct(out_shape, BF16),
        compiler_params=params("arbitrary"),
        cost_estimate=pl.CostEstimate(flops=flops, bytes_accessed=flops // 200, transcendentals=0),
        name=name,
    )(me, *fixed, *moving)


def total_kernel(parts_ref, grad_ref, squares_ref):
    total = parts_ref[0].astype(F32)
    for k in range(1, 16):
        total += parts_ref[k].astype(F32)
    grad_ref[...] = total
    squares = jnp.sum(total * total)
    squares_ref[...] = jnp.broadcast_to(squares, squares_ref.shape)


def total_rows(parts):
    return pl.pallas_call(
        total_kernel,
        out_shape=(
            jax.ShapeDtypeStruct((16, DO), F32),
            jax.ShapeDtypeStruct((128, 1, 128), F32),
        ),
        compiler_params=params(),
        name="total_rows",
    )(parts)


def adam_kernel(
    grad_ref, squares_ref, weight_ref, first_ref, fscale_ref, second_ref, sscale_ref,
    new_weight_ref, new_first_ref, new_fscale_ref, new_second_ref, new_sscale_ref,
):
    sum_squares = jnp.sum(squares_ref[:, 0, :]) * (1.0 / 128.0)
    rms = jnp.sqrt(jnp.full((16, GROUP), sum_squares * (1.0 / (QW * DO)) + 1e-06, F32))
    shrink = jnp.minimum(1.0, 1.0 / rms)

    def decode(coded, scale):
        magnitude = scale * jnp.sqrt(jnp.abs(coded))
        return jnp.where(coded < 0.0, -magnitude, magnitude)

    def encode(x):
        scale = jnp.max(jnp.abs(x), axis=-1, keepdims=True) + 1e-06
        return (x * jnp.abs(x) / (scale * scale)).astype(BF16), scale

    fscales, sscales = [], []
    for g in range(DO // GROUP):
        at = slice(g * GROUP, (g + 1) * GROUP)
        clipped = grad_ref[:, at] * shrink
        first_old = decode(first_ref[:, at].astype(F32), fscale_ref[:, g : g + 1])
        second_old = decode(second_ref[:, at].astype(F32), sscale_ref[:, g : g + 1])
        first = beta_first * first_old + (1.0 - beta_first) * clipped
        second = beta_second * second_old + (1.0 - beta_second) * clipped * clipped
        weight = weight_ref[:, at]
        new_weight_ref[:, at] = weight - learn_rate * (
            first / (jnp.sqrt(second) + 1e-08) + decay_rate * weight
        )
        new_first_ref[:, at], scale = encode(first)
        fscales.append(scale)
        new_second_ref[:, at], scale = encode(second)
        sscales.append(scale)
    new_fscale_ref[...] = jnp.concatenate(fscales, axis=1)
    new_sscale_ref[...] = jnp.concatenate(sscales, axis=1)


def adam(grad, squares, weight, first, fscale, second, sscale):
    return pl.pallas_call(
        adam_kernel,
        out_shape=tuple(
            jax.ShapeDtypeStruct(a.shape, a.dtype) for a in (weight, first, fscale, second, sscale)
        ),
        compiler_params=params(),
        name="adam",
    )(grad, squares, weight, first, fscale, second, sscale)


def shift(x, axis, by):
    peers = lax.axis_size(axis)
    return lax.ppermute(x, axis, [(i, (i + by) % peers) for i in range(peers)])


def after(x, earlier):
    return lax.optimization_barrier((x, earlier))[0]


def from_ring(mine):
    half = mine.shape[0] // 2
    left, right = shift(mine, "dp_0", 1), shift(mine, "dp_0", -1)
    top, bottom = shift(left[:half], "dp_0", 1), shift(right[half:], "dp_0", -1)
    return [mine, left, right, top, bottom]


def from_partner(arrays):
    return [shift(a, "dp_2", 1) for a in arrays]


def shift_y(x, by):
    pairs = []
    for y in range(4):
        to = (y + by) % 4
        pairs.append(((y % 2) * 2 + y // 2, (to % 2) * 2 + to // 2))
    return lax.ppermute(x, ("dp_1", "seq_1"), pairs)


def local(
    queries, keys, values, segments, cotangent, weight,
    first_moment, first_scale, second_moment, second_scale,
):
    me = jnp.stack([lax.axis_index(a) for a in DP_SEQ]).astype(jnp.int32)

    packed = pack(queries[0], keys[0], values[0], segments)
    arrived = lax.all_to_all(packed, SEQ, 0, 0, tiled=True)
    cots = from_ring(cotangent[0])

    attended = attend(arrived)
    own = lax.all_to_all(attended, SEQ, 0, 0, tiled=True)
    cots = cots + from_partner([after(a, attended) for a in cots])
    rows = after(weight.astype(BF16), attended)
    rows = jnp.concatenate([rows] + [shift_y(rows, k) for k in (1, 2, 3)], axis=0)

    columns = lax.all_to_all(own, ("dp_0", "dp_2"), 0, 0, tiled=True)
    rows = after(rows, own)
    rows = jnp.concatenate([rows] + [shift(rows, "seq_0", k) for k in (1, 2, 3)], axis=0)

    partial = over_columns(
        gradient_kernel, me, [columns], cots, (16, 16, WIDE), (16, 16, DO), "gradient_rows",
        2 * 256 * 2048 * DO,
    )
    rows = from_ring(after(rows, columns))
    parts = lax.all_to_all(partial, ("dp_1", "seq_0", "seq_1"), 0, 0, tiled=True)

    sums, squares = total_rows(parts)
    grad = lax.ppermute(sums, ("dp_1", "dp_2"), [(0, 0), (1, 2), (2, 1), (3, 3)])
    squares = lax.all_to_all(squares, DP_SEQ, 0, 0, tiled=True)
    rows = rows + from_partner(
        [after(a, partial) for a in rows[:3]] + [after(a, sums) for a in rows[3:]]
    )
    layer_out = over_columns(
        project_kernel, me, [own.reshape(8, 16, 16, TILE)], rows,
        (1, TILE, WIDE), (1, TILE, DO), "project", 1000,
    )
    new_weight, new_first, new_fscale, new_second, new_sscale = adam(
        after(grad, layer_out), squares, weight,
        first_moment, first_scale, second_moment, second_scale,
    )
    return (layer_out, new_weight, new_first, new_fscale, new_second, new_sscale)


def solution(mesh):
    finer = Mesh(mesh.devices.reshape(4, 2, 2, 4, 2), DP_SEQ)
    tokens = P(DP, SEQ, None)
    rows = P(DP_SEQ, None)
    return jax.shard_map(
        local,
        mesh=finer,
        in_specs=(tokens, tokens, tokens, P(DP, SEQ), tokens, rows, rows, rows, rows, rows),
        out_specs=(tokens, rows, rows, rows, rows, rows),
        check_vma=False,
    )
```

```python
import jax
import jax.numpy as jnp
from jax import lax
from jax.experimental import pallas as pl
from jax.experimental.pallas import tpu as pltpu
from jax.sharding import Mesh
from jax.sharding import PartitionSpec as P

QW = 2048
DO = 2304
GROUP = 128
TILE = 256
BLOCKS = 8
NOTE = 16
WIDE = 1152
ORDER = (0, 1, 3, 2)
SEQ = ("seq_0", "seq_1")
DP = ("dp_0", "dp_1", "dp_2")
DP_SEQ = ("dp_0", "dp_1", "dp_2", "seq_0", "seq_1")
LOG2E = 1.4426950408889634
VMEM_LIMIT = 60 * 1024 * 1024

score_scale = 144.0 ** (-0.5)
soft_cap = 50.0
beta_first = 0.9
beta_second = 0.95
learn_rate = 0.001
decay_rate = 0.1

F32 = jnp.float32
BF16 = jnp.bfloat16


def params(*semantics):
    return pltpu.CompilerParams(
        vmem_limit_bytes=VMEM_LIMIT,
        dimension_semantics=semantics or None,
    )


def restored(entries):
    wide = entries.astype(F32)
    scale = (jnp.max(jnp.abs(wide), axis=-1, keepdims=True) + 1e-06).astype(BF16).astype(F32)
    coded = (wide / scale).astype(BF16).astype(F32)
    return (coded * scale).astype(BF16)


def pack_kernel(q_ref, k_ref, v_ref, seg_ref, out_ref):
    seg = seg_ref[...]
    below_1 = jnp.sum((seg < 1).astype(F32), axis=-1, keepdims=True)
    below_2 = jnp.sum((seg < 2).astype(F32), axis=-1, keepdims=True)
    notes = jnp.concatenate(
        [jnp.broadcast_to(b, (NOTE, 256)) for b in (below_1, below_2)], axis=1
    ).astype(BF16)
    for h in range(BLOCKS):
        out_ref[h, :TILE, 0:256] = q_ref[:, h * 256 : (h + 1) * 256]
        out_ref[h, :TILE, 256:384] = restored(k_ref[:, h * 128 : (h + 1) * 128])
        out_ref[h, :TILE, 384:512] = restored(v_ref[:, h * 128 : (h + 1) * 128])
        out_ref[h, TILE:, :] = notes


def pack(q, k, v, seg):
    return pl.pallas_call(
        pack_kernel,
        out_shape=jax.ShapeDtypeStruct((BLOCKS, TILE + NOTE, 512), BF16),
        compiler_params=params(),
        cost_estimate=pl.CostEstimate(flops=0, bytes_accessed=6_000_000, transcendentals=0),
        name="pack",
    )(q, k, v, seg)


def attend_kernel(in_ref, out_ref):
    notes = in_ref[:, TILE : TILE + 8, :].astype(F32).sum(axis=0)
    first_of_1 = jnp.max(notes[:, 0:128]).astype(jnp.int32)
    first_of_2 = jnp.max(notes[:, 256:384]).astype(jnp.int32)

    def first_seen(place):
        return jnp.where(
            place < first_of_1, 0, jnp.where(place < first_of_2, first_of_1, first_of_2)
        )

    def tile(i, low):
        lane = lax.broadcasted_iota(jnp.int32, (1, 2 * TILE), 1)
        place = jnp.where(lane < TILE, lane, lane - TILE) + i * TILE
        seen = range(low, i + 1)
        query = jnp.concatenate([in_ref[i, :TILE, 0:128], in_ref[i, :TILE, 128:256]], axis=0)
        key = jnp.concatenate([in_ref[j, :TILE, 256:384] for j in seen], axis=0)
        value = jnp.concatenate([in_ref[j, :TILE, 384:512] for j in seen], axis=0)
        key_place = lax.broadcasted_iota(jnp.int32, (len(seen) * TILE, 2 * TILE), 0) + low * TILE
        scores = lax.dot_general(key, query, (((1,), (1,)), ((), ())), preferred_element_type=F32)
        capped = jnp.tanh(scores * (score_scale / soft_cap))
        weights = jnp.exp2(capped * (soft_cap * LOG2E))
        weights = jnp.where((key_place >= first_seen(place)) & (key_place <= place), weights, 0.0)
        total = jnp.sum(weights, axis=0, keepdims=True)
        mixed = lax.dot_general(
            value, weights.astype(BF16), (((0,), (0,)), ((), ())), preferred_element_type=F32
        )
        attended = (mixed / total).astype(BF16)
        for c in range(2):
            out_ref[i, c * 128 : (c + 1) * 128] = attended[:, c * TILE : (c + 1) * TILE]

    for i in range(BLOCKS):
        first = first_seen(jnp.int32(i * TILE)) // TILE
        for low in range(max(0, i - 5), i + 1):
            pl.when(first == low)(lambda i=i, low=low: tile(i, low))


def attend(packed):
    return pl.pallas_call(
        attend_kernel,
        out_shape=jax.ShapeDtypeStruct((BLOCKS, 256, TILE), BF16),
        in_specs=[pl.BlockSpec(memory_space=pltpu.VMEM)],
        out_specs=pl.BlockSpec(memory_space=pltpu.VMEM),
        compiler_params=params(),
        cost_estimate=pl.CostEstimate(
            flops=10_000_000_000, bytes_accessed=4_000_000, transcendentals=0
        ),
        name="attend",
    )(packed)


def gradient_kernel(me_ref, att_ref, *refs):
    cots, out_ref, left = refs[:10], refs[10], refs[11]

    @pl.when(pl.program_id(0) == 0)
    def _():
        for core in range(2):
            mine = me_ref[2] if core == 0 else 1 - me_ref[2]
            for k, back in enumerate(ORDER):
                x = lax.rem(me_ref[0] + 4 - back, 4)
                low = core * 1024 + k * TILE
                left[:, low : low + TILE] = att_ref[x * 2 + mine]

    right = jnp.concatenate([r[...] for r in cots], axis=0)
    low = jnp.dot(left[...], right, preferred_element_type=F32).astype(BF16)
    out_ref[...] = low.reshape(16, 16, WIDE)


def project_kernel(me_ref, att_ref, *refs):
    rows, out_ref, left = refs[:10], refs[10], refs[11]
    x, c, z = me_ref[0], me_ref[2], me_ref[3]
    y = me_ref[4] * 2 + me_ref[1]

    @pl.when(pl.program_id(0) == 0)
    def _():
        for core in range(2):
            row_c = c if core == 0 else 1 - c
            for k, back in enumerate(ORDER):
                row_x = lax.rem(x + 4 - back, 4)
                blocks = []
                for back_z in range(4):
                    row_z = lax.rem(z + 4 - back_z, 4)
                    for back_y in range(4):
                        row_y = lax.rem(y + 4 - back_y, 4)
                        low, high = lax.rem(row_y, 2), row_y // 2
                        blocks.append(att_ref[row_x * 2 + low, row_c * 8 + row_z * 2 + high])
                at = core * 1024 + k * TILE
                left[:, at : at + TILE] = jnp.concatenate(blocks, axis=0).T

    right = jnp.concatenate([r[...] for r in rows], axis=0)
    out_ref[0] = jnp.dot(left[...], right, preferred_element_type=F32).astype(BF16)


def over_columns(kernel, me, fixed, moving, out_block, out_shape, name, flops):
    return pl.pallas_call(
        kernel,
        grid_spec=pltpu.PrefetchScalarGridSpec(
            num_scalar_prefetch=1,
            grid=(DO // WIDE,),
            in_specs=[pl.BlockSpec(a.shape, lambda n, me, d=a.ndim: (0,) * d) for a in fixed]
            + [pl.BlockSpec((a.shape[0], WIDE), lambda n, me: (0, n)) for a in moving],
            out_specs=pl.BlockSpec(out_block, lambda n, me: (0, 0, n)),
            scratch_shapes=[pltpu.VMEM((TILE, 2048), BF16)],
        ),
        out_shape=jax.ShapeDtypeStruct(out_shape, BF16),
        compiler_params=params("arbitrary"),
        cost_estimate=pl.CostEstimate(flops=flops, bytes_accessed=flops // 200, transcendentals=0),
        name=name,
    )(me, *fixed, *moving)


def total_kernel(parts_ref, grad_ref, squares_ref):
    total = parts_ref[0].astype(F32)
    for k in range(1, 16):
        total += parts_ref[k].astype(F32)
    grad_ref[...] = total
    squares = jnp.sum(total * total)
    squares_ref[...] = jnp.broadcast_to(squares, squares_ref.shape)


def total_rows(parts):
    return pl.pallas_call(
        total_kernel,
        out_shape=(
            jax.ShapeDtypeStruct((16, DO), F32),
            jax.ShapeDtypeStruct((128, 1, 128), F32),
        ),
        compiler_params=params(),
        name="total_rows",
    )(parts)


def adam_kernel(
    grad_ref, squares_ref, weight_ref, first_ref, fscale_ref, second_ref, sscale_ref,
    new_weight_ref, new_first_ref, new_fscale_ref, new_second_ref, new_sscale_ref,
):
    sum_squares = jnp.sum(squares_ref[:, 0, :]) * (1.0 / 128.0)
    rms = jnp.sqrt(jnp.full((16, GROUP), sum_squares * (1.0 / (QW * DO)) + 1e-06, F32))
    shrink = jnp.minimum(1.0, 1.0 / rms)

    def decode(coded, scale):
        magnitude = scale * jnp.sqrt(jnp.abs(coded))
        return jnp.where(coded < 0.0, -magnitude, magnitude)

    def encode(x):
        scale = jnp.max(jnp.abs(x), axis=-1, keepdims=True) + 1e-06
        return (x * jnp.abs(x) / (scale * scale)).astype(BF16), scale

    fscales, sscales = [], []
    for g in range(DO // GROUP):
        at = slice(g * GROUP, (g + 1) * GROUP)
        clipped = grad_ref[:, at] * shrink
        first_old = decode(first_ref[:, at].astype(F32), fscale_ref[:, g : g + 1])
        second_old = decode(second_ref[:, at].astype(F32), sscale_ref[:, g : g + 1])
        first = beta_first * first_old + (1.0 - beta_first) * clipped
        second = beta_second * second_old + (1.0 - beta_second) * clipped * clipped
        weight = weight_ref[:, at]
        new_weight_ref[:, at] = weight - learn_rate * (
            first / (jnp.sqrt(second) + 1e-08) + decay_rate * weight
        )
        new_first_ref[:, at], scale = encode(first)
        fscales.append(scale)
        new_second_ref[:, at], scale = encode(second)
        sscales.append(scale)
    new_fscale_ref[...] = jnp.concatenate(fscales, axis=1)
    new_sscale_ref[...] = jnp.concatenate(sscales, axis=1)


def adam(grad, squares, weight, first, fscale, second, sscale):
    return pl.pallas_call(
        adam_kernel,
        out_shape=tuple(
            jax.ShapeDtypeStruct(a.shape, a.dtype) for a in (weight, first, fscale, second, sscale)
        ),
        compiler_params=params(),
        cost_estimate=pl.CostEstimate(
            flops=30_000_000_000, bytes_accessed=1_000_000, transcendentals=0
        ),
        name="adam",
    )(grad, squares, weight, first, fscale, second, sscale)


def shift(x, axis, by):
    peers = lax.axis_size(axis)
    return lax.ppermute(x, axis, [(i, (i + by) % peers) for i in range(peers)])


def after(x, earlier):
    return lax.optimization_barrier((x, earlier))[0]


def from_ring(mine):
    half = mine.shape[0] // 2
    left, right = shift(mine, "dp_0", 1), shift(mine, "dp_0", -1)
    top, bottom = shift(left[:half], "dp_0", 1), shift(right[half:], "dp_0", -1)
    return [mine, left, right, top, bottom]


def from_partner(arrays):
    return [shift(a, "dp_2", 1) for a in arrays]


def shift_y(x, by):
    pairs = []
    for y in range(4):
        to = (y + by) % 4
        pairs.append(((y % 2) * 2 + y // 2, (to % 2) * 2 + to // 2))
    return lax.ppermute(x, ("dp_1", "seq_1"), pairs)


def local(
    queries, keys, values, segments, cotangent, weight,
    first_moment, first_scale, second_moment, second_scale,
):
    me = jnp.stack([lax.axis_index(a) for a in DP_SEQ]).astype(jnp.int32)

    packed = pack(queries[0], keys[0], values[0], segments)
    arrived = lax.all_to_all(packed, SEQ, 0, 0, tiled=True)
    cots = from_ring(cotangent[0])

    attended = attend(arrived)
    own = lax.all_to_all(attended, SEQ, 0, 0, tiled=True)
    cots = cots + from_partner([after(a, attended) for a in cots])
    rows = after(weight.astype(BF16), attended)
    rows = jnp.concatenate([rows] + [shift_y(rows, k) for k in (1, 2, 3)], axis=0)

    columns = lax.all_to_all(own, ("dp_0", "dp_2"), 0, 0, tiled=True)
    rows = after(rows, own)
    rows = jnp.concatenate([rows] + [shift(rows, "seq_0", k) for k in (1, 2, 3)], axis=0)

    partial = over_columns(
        gradient_kernel, me, [columns], cots, (16, 16, WIDE), (16, 16, DO), "gradient_rows",
        2 * 256 * 2048 * DO,
    )
    rows = from_ring(after(rows, columns))
    parts = lax.all_to_all(partial, ("dp_1", "seq_0", "seq_1"), 0, 0, tiled=True)

    sums, squares = total_rows(parts)
    grad = lax.ppermute(sums, ("dp_1", "dp_2"), [(0, 0), (1, 2), (2, 1), (3, 3)])
    squares = lax.all_to_all(squares, DP_SEQ, 0, 0, tiled=True)
    rows = rows + from_partner(
        [after(a, partial) for a in rows[:3]] + [after(a, squares) for a in rows[3:]]
    )
    layer_out = over_columns(
        project_kernel, me, [own.reshape(8, 16, 16, TILE)], rows,
        (1, TILE, WIDE), (1, TILE, DO), "project", 1000,
    )
    new_weight, new_first, new_fscale, new_second, new_sscale = adam(
        grad, squares, weight,
        first_moment, first_scale, second_moment, second_scale,
    )
    return (layer_out, new_weight, new_first, new_fscale, new_second, new_sscale)


def solution(mesh):
    finer = Mesh(mesh.devices.reshape(4, 2, 2, 4, 2), DP_SEQ)
    tokens = P(DP, SEQ, None)
    rows = P(DP_SEQ, None)
    return jax.shard_map(
        local,
        mesh=finer,
        in_specs=(tokens, tokens, tokens, P(DP, SEQ), tokens, rows, rows, rows, rows, rows),
        out_specs=(tokens, rows, rows, rows, rows, rows),
        check_vma=False,
    )
```
